32 devices in a mesh: groups: 2 (over x), node: 2 (over core), local: 8 (over z, y).
Axes of the slice: x: 2, y: 2, z: 4, core: 2. Of those that a mesh axis runs over, the one named last changes fastest.
Arguments:
- tokens: bfloat16 [256, 7168], P(('groups', 'node', 'local')), parts along dimension 0, may hold values from -6 to 6
- expert_ids: int32 [256, 8], P(('groups', 'node', 'local')), parts along dimension 0, may hold values from 0 to 15, all different within a row; in each aligned block of 8 rows (0 to 7, 8 to 15, ...) at most 6 rows name the same one
- route_weights: bfloat16 [256, 8], P(('groups', 'node', 'local')), parts along dimension 0, may hold values from 0.049804688 to 1
- w_gate: bfloat16 [16, 7168, 1024], P(('node', 'local')), may hold values from -0.0625 to 0.0625
- w_up: bfloat16 [16, 7168, 1024], P(('node', 'local')), may hold values from -0.0625 to 0.0625
- w_down: bfloat16 [16, 1024, 7168], P(('node', 'local')), may hold values from -0.1875 to 0.1875
Outputs:
- layer_out: bfloat16 [256, 7168], P(('groups', 'node', 'local')), parts along dimension 0
The draws below stay inside these ranges and needn't reach their ends.
There are 2 independent parts, one for each index of `groups`. The reference program is written for one: setup_inputs(seed, part) draws one part's arguments, and reference() takes and returns one part's arrays. A program takes and returns all parts, laid end to end along the dimension named above; an argument that names none is the same for every part. Nothing has to cross between parts.
Inputs may be any that keep to these rules, and one draw needn't show every extreme that they name: `expert_ids`: each row names 8 different experts; among the 8 rows of one device no expert is named by more than 6 rows, and in every draw some expert is named by exactly 6 rows of some device.
All inputs are finite; a program needn't handle non-finite values.
Results may differ from the reference program's by a relative error of at most 0.0057.
Values may be sent and summed in bfloat16 or wider, within the bound.
No kernel may reach another device: no remote copies, remote signals or barrier semaphores. Data moves between devices by JAX's collectives and lax.ppermute only.
A program may use at most 128 MiB of HBM per device.

```python
import math
import jax
import jax.numpy as jnp
import numpy as np
from jax import lax

D = 7168
HID = 1024
EXPERTS = 16
TOP = 8
TOK_DEV = 8
CAP = 6
SPLIT = 1
HID_DEV = 1024
SLICES = 16
TOKENS = 128


def steps_of(rng, extent, split, least, largest):
    def one(dim, shards_of):
        heights = jax.random.uniform(jax.random.fold_in(jax.random.fold_in(rng, 6), dim), (shards_of,), jnp.float32, least / len(split), largest / len(split))
        return jnp.repeat(jnp.exp(heights), extent[dim] // shards_of).reshape((-1,) + (1,) * (len(extent) - dim - 1))

    gain = one(*split[0])
    for cut in split[1:]:
        gain = gain * one(*cut)
    return gain


def deal_out(own_key, own, number, rows, amount, top, most, lean):
    order = jax.random.permutation(own_key, amount)
    packed, common = load_shares(amount, rows * top, most, lean, True), load_shares(amount, rows * top, most, lean, False)
    places = jnp.arange(amount)

    def named(tallies, turn):
        used = int((tallies > 0).sum())
        fixed = max(1, used // 4)
        moved = fixed + (places - fixed + turn * (used - fixed)) % max(1, amount - fixed)
        return jnp.zeros((amount,), jnp.int32).at[order[jnp.where(places < fixed, places, moved)]].set(jnp.asarray(tallies, jnp.int32))

    tallies = jnp.where(number % 4 == 0, named(packed, number // 4), named(common, number - number // 4 - 1))
    mixed = jax.random.permutation(jax.random.fold_in(own, 3), amount)
    donor, sink = mixed[0:amount // 2 * 2:2], mixed[1:amount // 2 * 2:2]
    slack = jnp.minimum(tallies[donor] - 1, most - tallies[sink]) // 2
    slack = jnp.where((donor == order[0]) | (sink == order[0]) | (tallies[sink] == 0), 0, jnp.maximum(slack, 0))
    moved = jax.random.randint(jax.random.fold_in(own, 4), (amount // 2,), 0, 1 << 20) % (slack + 1)
    tallies = tallies.at[donor].add(-moved).at[sink].add(moved)
    members = jnp.searchsorted(jnp.cumsum(tallies), jnp.arange(rows * top), side="right").astype(jnp.int32)
    grid = members.reshape(top, rows).T
    grid = grid[jax.random.permutation(jax.random.fold_in(own, 1), rows)]
    turn = jax.random.randint(jax.random.fold_in(own, 2), (rows, 1), 0, top)
    return jnp.take_along_axis(grid, (jnp.arange(top)[None, :] + turn) % top, axis=1)


def load_shares(number_of, total, most, lean, full):
    portions = [(1 << 20) // math.isqrt(grade ** lean) + 1 for grade in range(1, number_of + 1)]
    largest = most if full else min(most, max(-(-total // number_of), total * portions[0] // sum(portions)))
    least = 1 if total - largest >= number_of - 1 else 0
    holding, surplus = [largest] + [least] * (number_of - 1), total - largest - least * (number_of - 1)
    while surplus > 0:
        movable = [i for i in range(1, number_of) if holding[i] < largest] or [i for i in range(1, number_of) if holding[i] < most]
        mass, left = sum([portions[i] for i in movable]), surplus
        for i in movable:
            extra = min(most - holding[i], max(1, left * portions[i] // mass), surplus)
            holding[i] = holding[i] + extra
            surplus = surplus - extra
    return np.array(holding)


def scatter_about(rng, shape, width, reach, cuts=(), kind=jnp.bfloat16):
    values = jax.random.normal(rng, shape, jnp.float32) * width
    if len(cuts) > 0:
        values = steps_of(rng, shape, cuts, -0.22, 0.18) * values
    return jnp.clip(values, min=-reach, max=reach).astype(kind)


def setup_inputs(seed: int = 0, part: int = 0) -> dict:
    keys = jax.random.split(jax.random.key(seed), 7)
    own_keys = jax.random.split(jax.random.fold_in(keys[6], part), 7)
    tokens = scatter_about(own_keys[0], (TOKENS, D), 1.0, 6.0, ((0, 16),))
    expert_ids_keys = jax.random.split(jax.random.fold_in(own_keys[1], 1), TOKENS // TOK_DEV)
    expert_ids_turns = jax.random.permutation(jax.random.fold_in(own_keys[1], 3), TOKENS // TOK_DEV)
    expert_ids = jax.vmap(lambda own, number: deal_out(jax.random.fold_in(own_keys[1], 2), own, number, TOK_DEV, EXPERTS, TOP, CAP, 2))(expert_ids_keys, expert_ids_turns).reshape((TOKENS, TOP))
    route_weights = jnp.clip(jnp.exp(math.log(1.0) - 2.9996462 * jax.random.uniform(own_keys[2], (TOKENS, TOP), jnp.float32) ** steps_of(own_keys[2], (TOKENS, TOP), ((0, 16),), -0.2, 0.2)), 0.049804688, 1.0).astype(jnp.bfloat16)
    w_gate = scatter_about(keys[3], (SLICES, D, HID_DEV), D ** -0.5, 0.0625, ((0, 16),))
    w_up = scatter_about(keys[4], (SLICES, D, HID_DEV), D ** -0.5, 0.0625, ((0, 16),))
    w_down = scatter_about(keys[5], (SLICES, HID_DEV, D), HID ** -0.5, 0.1875, ((0, 16),))
    return dict(tokens=tokens, expert_ids=expert_ids, route_weights=route_weights, w_gate=w_gate, w_up=w_up, w_down=w_down)


def reference(tokens, expert_ids, route_weights, w_gate, w_up, w_down):
    chosen = (expert_ids[:, :, None] == jnp.arange(EXPERTS, dtype=jnp.int32)[None, None, :]).astype(jnp.float32)
    coefficient = jnp.sum(route_weights.astype(jnp.float32)[:, :, None] * chosen, axis=1)

    def one_expert(carry, expert_index):
        total = jnp.zeros((TOKENS, D), jnp.float32)
        for slice_offset in range(SPLIT):
            slice_index = (expert_index * SPLIT + slice_offset).astype(jnp.int32)
            gate_proj = lax.dynamic_index_in_dim(w_gate, slice_index, 0, keepdims=False)
            up_proj = lax.dynamic_index_in_dim(w_up, slice_index, 0, keepdims=False)
            down_proj = lax.dynamic_index_in_dim(w_down, slice_index, 0, keepdims=False)
            gate_val = jnp.dot(tokens, gate_proj, preferred_element_type=jnp.float32)
            up_val = jnp.dot(tokens, up_proj, preferred_element_type=jnp.float32)
            hidden = (jax.nn.silu(gate_val) * up_val).astype(jnp.bfloat16)
            partial_out = jnp.dot(hidden, down_proj, preferred_element_type=jnp.float32).astype(jnp.bfloat16)
            total = total + partial_out.astype(jnp.float32)
        expert_out = total.astype(jnp.bfloat16)
        weight_col = lax.dynamic_slice_in_dim(coefficient, expert_index, 1, 1)
        return carry + weight_col * expert_out.astype(jnp.float32), None

    result, unused = lax.scan(one_expert, jnp.zeros((TOKENS, D), jnp.float32), jnp.arange(EXPERTS, dtype=jnp.int32))
    return result.astype(jnp.bfloat16)
```

```python
import functools

import jax
import jax.numpy as jnp
from jax import lax
from jax.experimental import pallas as pl
from jax.experimental.pallas import tpu as pltpu
from jax.sharding import PartitionSpec as P

EXPERTS = 16
LANES = 128
GATHER_CHUNKS = 2
RETURN_CHUNKS = 2
VM = pltpu.VMEM
F32 = jnp.float32
BF16 = jnp.bfloat16


def in_vmem(array):
    return pltpu.with_memory_space_constraint(array, VM)


def call(kernel, outs, *args, limit, flops, nbytes):
    return pl.pallas_call(
        kernel,
        out_shape=outs,
        in_specs=[pl.BlockSpec(memory_space=VM)] * len(args),
        out_specs=jax.tree.map(lambda _: pl.BlockSpec(memory_space=VM), outs),
        compiler_params=pltpu.CompilerParams(vmem_limit_bytes=limit * 2**20),
        cost_estimate=pl.CostEstimate(
            flops=flops, bytes_accessed=nbytes, transcendentals=0
        ),
    )(*args)


def level_bits(node_count, bits):
    even = list(range(bits - 1, -1, -1))
    odd = even[:-2] + even[-2:][::-1]
    return [[(even, odd)[n % 2][k] for n in range(node_count)] for k in range(bits)]


def swap(array, level, local_count):
    perm = [
        (n * local_count + i, n * local_count + (i ^ (1 << bit)))
        for n, bit in enumerate(level)
        for i in range(local_count)
    ]
    return lax.ppermute(array, ("node", "local"), perm)


def swap_core(array, node_count):
    return lax.ppermute(array, "node", [(n, n ^ 1) for n in range(node_count)])


def proj_kernel(lo, hi, first, last, *refs):
    if first:
        own, other, w_gate, w_up = refs[:4]
        outs = refs[4:]
        gate = up = None
    else:
        own, other, w_gate, w_up, gate_in, up_in = refs[:6]
        outs = refs[6:]
        gate, up = gate_in[...], up_in[...]
    step = 512 if (hi - lo) % 512 == 0 else LANES
    for c in range(lo, hi, step):
        rows = jnp.concatenate(
            [own[:, c - lo : c - lo + step], other[:, c - lo : c - lo + step]], axis=0
        )
        g = jnp.dot(rows, w_gate[0, c : c + step, :], preferred_element_type=F32)
        u = jnp.dot(rows, w_up[0, c : c + step, :], preferred_element_type=F32)
        gate = g if gate is None else gate + g
        up = u if up is None else up + u
    if last:
        outs[0][...] = (gate / (1.0 + jnp.exp(-gate)) * up).astype(BF16)
    else:
        outs[0][...] = gate
        outs[1][...] = up


def down_kernel(lo, hi, hidden, own_coef, other_coef, pick, w_down, own_out, other_out):
    half = own_out.shape[0]
    coef = jnp.concatenate([own_coef[...], other_coef[...]], axis=0).astype(F32)
    coef = jnp.sum(coef * pick[...], axis=1, keepdims=True)
    step = 512 if (hi - lo) % 512 == 0 else LANES
    h = hidden[...]
    for c in range(lo, hi, step):
        part = coef * jnp.dot(
            h, w_down[0, :, c : c + step], preferred_element_type=F32
        )
        own_out[:, c - lo : c - lo + step] = part[:half]
        other_out[:, c - lo : c - lo + step] = part[half:].astype(BF16)


def edges(width, chunks):
    tiles = width // LANES
    return [tiles * i // chunks * LANES for i in range(chunks + 1)]


def shards(tokens, expert_ids, route_weights, w_gate, w_up, w_down):
    tok_rows, width = tokens.shape
    hid = w_gate.shape[2]
    node_count = lax.axis_size("node")
    local_count = lax.axis_size("local")
    split_count = node_count * local_count // EXPERTS
    bits = local_count.bit_length() - 1
    levels = level_bits(node_count, bits)
    half = tok_rows * local_count
    rows = 2 * half
    me = lax.axis_index("node") * local_count + lax.axis_index("local")
    pick = (jnp.arange(LANES, dtype=jnp.int32)[None, :] == me // split_count).astype(F32)
    hits = expert_ids[:, :, None] == jnp.arange(LANES, dtype=jnp.int32)[None, None, :]
    coef = jnp.sum(
        jnp.where(hits, route_weights.astype(F32)[:, :, None], 0.0), axis=1
    ).astype(BF16)

    cuts = edges(width, GATHER_CHUNKS)
    blocks = [tokens[:, a:b] for a, b in zip(cuts, cuts[1:])]
    blocks[-1] = jnp.concatenate([blocks[-1], coef], axis=1)
    for level in levels:
        blocks = [
            jnp.concatenate([b, swap(b, level, local_count)], axis=0) for b in blocks
        ]
    others = [swap_core(b, node_count) for b in blocks]

    w_gate, w_up, w_down = in_vmem(w_gate), in_vmem(w_up), in_vmem(w_down)
    state = ()
    for i, (a, b) in enumerate(zip(cuts, cuts[1:])):
        first, last = i == 0, i == GATHER_CHUNKS - 1
        outs = (
            [VM((rows, hid), BF16)] if last else [VM((rows, hid), F32)] * 2
        )
        state = call(
            functools.partial(proj_kernel, a, b, first, last),
            outs,
            blocks[i],
            others[i],
            w_gate,
            w_up,
            *state,
            limit=8,
            flops=4 * rows * hid * (b - a),
            nbytes=4 * hid * (b - a),
        )
    hidden = state[0]
    own_coef, other_coef = blocks[-1][:, -LANES:], others[-1][:, -LANES:]

    cuts = edges(width, RETURN_CHUNKS)
    results = []
    for a, b in zip(cuts, cuts[1:]):
        own, other = call(
            functools.partial(down_kernel, a, b),
            [VM((half, b - a), F32), VM((half, b - a), BF16)],
            hidden,
            own_coef,
            other_coef,
            pick,
            w_down,
            limit=8,
            flops=2 * rows * hid * (b - a),
            nbytes=2 * hid * (b - a),
        )
        total = own + swap_core(other, node_count).astype(F32)
        for level in levels[::-1]:
            n = total.shape[0] // 2
            total = total[:n] + swap(total[n:].astype(BF16), level, local_count).astype(
                F32
            )
        results.append(total.astype(BF16))
    return jnp.concatenate(results, axis=1)


def solution(mesh):
    return jax.shard_map(
        shards,
        mesh=mesh,
        in_specs=(
            P(("groups", "node", "local"), None),
            P(("groups", "node", "local"), None),
            P(("groups", "node", "local"), None),
            P(("node", "local"), None, None),
            P(("node", "local"), None, None),
            P(("node", "local"), None, None),
        ),
        out_specs=P(("groups", "node", "local"), None),
        check_vma=False,
    )
```

```python
import functools

import jax
import jax.numpy as jnp
from jax import lax
from jax.experimental import pallas as pl
from jax.experimental.pallas import tpu as pltpu
from jax.sharding import PartitionSpec as P

EXPERTS = 16
LANES = 128
GATHER_CHUNKS = 2
RETURN_CHUNKS = 2
QUARTERS = 4
VM = pltpu.VMEM
F32 = jnp.float32
BF16 = jnp.bfloat16


def in_vmem(array):
    return pltpu.with_memory_space_constraint(array, VM)


def in_hbm(array):
    return pltpu.with_memory_space_constraint(array, pltpu.HBM)


def call(kernel, outs, *args, limit, flops, nbytes, scalars=(), after=()):
    def body(*refs):
        kernel(*refs[: len(scalars)], *refs[len(scalars) + len(after) :])

    return pl.pallas_call(
        body,
        out_shape=outs,
        in_specs=[pl.BlockSpec(memory_space=pltpu.SMEM)] * len(scalars)
        + [pl.BlockSpec(memory_space=pl.ANY)] * len(after)
        + [pl.BlockSpec(memory_space=VM)] * len(args),
        out_specs=[pl.BlockSpec(memory_space=VM)] * len(outs),
        compiler_params=pltpu.CompilerParams(vmem_limit_bytes=limit * 2**20),
        cost_estimate=pl.CostEstimate(
            flops=flops, bytes_accessed=nbytes, transcendentals=0
        ),
    )(*scalars, *after, *args)


def load_rows(arrays, lo, hi, after):
    count = len(arrays)

    def body(_, *refs):
        sems = refs[-1]
        copies = [
            pltpu.make_async_copy(
                refs[i].at[0, pl.ds(lo, hi - lo)], refs[count + i], sems.at[i]
            )
            for i in range(count)
        ]
        for copy in copies:
            copy.start()
        for copy in copies:
            copy.wait()

    outs = [VM((hi - lo, x.shape[2]), BF16) for x in arrays]
    return pl.pallas_call(
        body,
        out_shape=outs,
        in_specs=[pl.BlockSpec(memory_space=pl.ANY)]
        + [pl.BlockSpec(memory_space=pltpu.HBM)] * count,
        out_specs=[pl.BlockSpec(memory_space=VM)] * count,
        scratch_shapes=[pltpu.SemaphoreType.DMA((count,))],
        compiler_params=pltpu.CompilerParams(vmem_limit_bytes=2**20),
        cost_estimate=pl.CostEstimate(
            flops=0,
            bytes_accessed=2 * (hi - lo) * sum(x.shape[2] for x in arrays),
            transcendentals=0,
        ),
    )(after, *[in_hbm(x) for x in arrays])


def level_bits(node_count, bits):
    even = list(range(bits - 1, -1, -1))
    odd = even[:-2] + even[-2:][::-1]
    return [[(even, odd)[n % 2][k] for n in range(node_count)] for k in range(bits)]


def swap(array, level, local_count):
    perm = [
        (n * local_count + i, n * local_count + (i ^ (1 << bit)))
        for n, bit in enumerate(level)
        for i in range(local_count)
    ]
    return lax.ppermute(array, ("node", "local"), perm)


def swap_core(array, node_count):
    return lax.ppermute(array, "node", [(n, n ^ 1) for n in range(node_count)])


def prepare_kernel(tokens, ids, weights, out):
    width = tokens.shape[1]
    lane = lax.broadcasted_iota(jnp.int32, (tokens.shape[0], LANES), 1)
    coef = jnp.zeros((tokens.shape[0], LANES), F32)
    for k in range(ids.shape[1]):
        named = weights[:, k : k + 1].astype(F32)
        coef = coef + jnp.where(lane == ids[:, k : k + 1], named, 0.0)
    out[:, :width] = tokens[...]
    out[:, width:] = coef.astype(BF16)


def join_kernel(cuts, own, other, *outs):
    for out, a, b in zip(outs, cuts, cuts[1:]):
        rows = [own[:, a:b].astype(F32), other[:, a:b].astype(F32)]
        out[...] = jnp.concatenate(rows, axis=0).astype(BF16)


def proj_kernel(pieces, last, *refs):
    count = len(pieces) - 1
    weights, refs = refs[: 2 * count], refs[2 * count :]
    parts, refs = refs[:4], refs[4:]
    gate = up = None
    if not (pieces[0] == 0):
        gate, up = refs[0][...], refs[1][...]
        refs = refs[2:]
    for i, (lo, hi) in enumerate(zip(pieces, pieces[1:])):
        step = 896 if (hi - lo) % 896 == 0 else LANES
        for c in range(0, hi - lo, step):
            at = lo - pieces[0] + c
            rows = jnp.concatenate([p[:, at : at + step] for p in parts], axis=0)
            g = jnp.dot(
                rows, weights[2 * i][c : c + step, :], preferred_element_type=F32
            )
            u = jnp.dot(
                rows, weights[2 * i + 1][c : c + step, :], preferred_element_type=F32
            )
            gate = g if gate is None else gate + g
            up = u if up is None else up + u
    if last:
        refs[0][...] = (gate / (1.0 + jnp.exp(-gate)) * up).astype(BF16)
    else:
        refs[0][...] = gate
        refs[1][...] = up


def down_kernel(lo, hi, expert, w_down, hidden, *refs):
    parts, (own_out, other_out) = refs[:-2], refs[-2:]
    half = own_out.shape[0]
    coef = jnp.concatenate([p[:, -LANES:] for p in parts], axis=0).astype(F32)
    lane = lax.broadcasted_iota(jnp.int32, coef.shape, 1)
    coef = jnp.sum(jnp.where(lane == expert[0], coef, 0.0), axis=1, keepdims=True)
    step = 512 if (hi - lo) % 512 == 0 else LANES
    h = hidden[...]
    for c in range(lo, hi, step):
        part = coef * jnp.dot(
            h, w_down[0, :, c : c + step], preferred_element_type=F32
        )
        own_out[:, c - lo : c - lo + step] = part[:half]
        other_out[:, c - lo : c - lo + step] = part[half:].astype(BF16)


def edges(width, chunks):
    tiles = width // LANES
    return [tiles * i // chunks * LANES for i in range(chunks + 1)]


def shards(tokens, expert_ids, route_weights, w_gate, w_up, w_down):
    tok_rows, width = tokens.shape
    hid = w_gate.shape[2]
    node_count = lax.axis_size("node")
    local_count = lax.axis_size("local")
    split_count = node_count * local_count // EXPERTS
    bits = local_count.bit_length() - 1
    levels = level_bits(node_count, bits)
    half = tok_rows * local_count
    rows = 2 * half
    me = lax.axis_index("node") * local_count + lax.axis_index("local")
    expert = (me // split_count).astype(jnp.int32).reshape(1)

    block = call(
        lambda _, *refs: prepare_kernel(*refs),
        [VM((tok_rows, width + LANES), BF16)],
        tokens,
        expert_ids,
        route_weights,
        scalars=(expert,),
        limit=2,
        flops=0,
        nbytes=200_000,
    )[0]
    quarters = edges(width, QUARTERS)
    spans = list(zip(quarters, quarters[1:]))
    loads = [[0, 1], [2], [3]]
    loaded = {}

    def load(k, after):
        for q in loads[k] if k < len(loads) else []:
            loaded[q] = load_rows((w_gate, w_up), *spans[q], after)
        return [loaded[q][0] for q in (loads[k] if k < len(loads) else [])]

    cuts = edges(width, GATHER_CHUNKS)
    wide = cuts[:-1] + [cuts[-1] + LANES]
    for k, level in enumerate(levels[:-1]):
        other = swap(block, level, local_count)
        ties = load(k, block)
        ends = wide if k == bits - 2 else [0, width + LANES]
        blocks = call(
            functools.partial(join_kernel, ends),
            [VM((2 * block.shape[0], b - a), BF16) for a, b in zip(ends, ends[1:])],
            block,
            other,
            after=ties,
            limit=4,
            flops=0,
            nbytes=200_000,
        )
        block = blocks[0]
    for q in range(len(spans)):
        if q not in loaded:
            loaded[q] = load_rows((w_gate, w_up), *spans[q], block)
    parts = []
    for b in blocks:
        far = swap(b, levels[-1], local_count)
        parts.append([b, far, swap_core(b, node_count), swap_core(far, node_count)])

    w_down = in_vmem(w_down)
    state = ()
    each = QUARTERS // GATHER_CHUNKS
    for i in range(GATHER_CHUNKS):
        last = i == GATHER_CHUNKS - 1
        use = range(i * each, (i + 1) * each)
        state = call(
            functools.partial(
                proj_kernel, quarters[i * each : (i + 1) * each + 1], last
            ),
            [VM((rows, hid), BF16)] if last else [VM((rows, hid), F32)] * 2,
            *[w for q in use for w in loaded[q]],
            *parts[i],
            *state,
            limit=8,
            flops=4 * rows * hid * (cuts[i + 1] - cuts[i]),
            nbytes=4 * hid * (cuts[i + 1] - cuts[i]),
        )
    hidden = state[0]

    cuts = edges(width, RETURN_CHUNKS)
    results = []
    for a, b in zip(cuts, cuts[1:]):
        own, other = call(
            functools.partial(down_kernel, a, b),
            [VM((half, b - a), F32), VM((half, b - a), BF16)],
            w_down,
            hidden,
            *parts[-1],
            scalars=(expert,),
            limit=8,
            flops=2 * rows * hid * (b - a),
            nbytes=2 * hid * (b - a),
        )
        total = own + swap_core(other, node_count).astype(F32)
        for level in levels[::-1]:
            n = total.shape[0] // 2
            total = total[:n] + swap(total[n:].astype(BF16), level, local_count).astype(
                F32
            )
        results.append(total.astype(BF16))
    return jnp.concatenate(results, axis=1)


def solution(mesh):
    return jax.shard_map(
        shards,
        mesh=mesh,
        in_specs=(
            P(("groups", "node", "local"), None),
            P(("groups", "node", "local"), None),
            P(("groups", "node", "local"), None),
            P(("node", "local"), None, None),
            P(("node", "local"), None, None),
            P(("node", "local"), None, None),
        ),
        out_specs=P(("groups", "node", "local"), None),
        check_vma=False,
    )
```

```python
import functools

import jax
import jax.numpy as jnp
from jax import lax
from jax.experimental import pallas as pl
from jax.experimental.pallas import tpu as pltpu
from jax.sharding import PartitionSpec as P

EXPERTS = 16
LANES = 128
GATHER_CHUNKS = 2
RETURN_CHUNKS = 2
VM = pltpu.VMEM
F32 = jnp.float32
BF16 = jnp.bfloat16


def in_vmem(array):
    return pltpu.with_memory_space_constraint(array, VM)


def in_hbm(array):
    return pltpu.with_memory_space_constraint(array, pltpu.HBM)


def call(kernel, outs, *args, limit, flops, nbytes, scalars=(), far=()):
    def body(*refs):
        kernel(*refs[: len(scalars)], *refs[len(scalars) + len(far) :])


    return pl.pallas_call(
        body,
        out_shape=outs,
        in_specs=[pl.BlockSpec(memory_space=pltpu.SMEM)] * len(scalars)
        + [pl.BlockSpec(memory_space=pltpu.HBM)] * len(far)
        + [pl.BlockSpec(memory_space=VM)] * len(args),
        out_specs=[pl.BlockSpec(memory_space=VM)] * len(outs),
        compiler_params=pltpu.CompilerParams(vmem_limit_bytes=limit * 2**20),
        cost_estimate=pl.CostEstimate(
            flops=flops, bytes_accessed=nbytes, transcendentals=0
        ),
    )(*scalars, *[in_hbm(x) for x in far], *args)


def level_bits(node_count, bits):
    even = list(range(bits - 1, -1, -1))
    odd = even[:-2] + even[-2:][::-1]
    return [[(even, odd)[n % 2][k] for n in range(node_count)] for k in range(bits)]


def swap(array, level, local_count):
    perm = [
        (n * local_count + i, n * local_count + (i ^ (1 << bit)))
        for n, bit in enumerate(level)
        for i in range(local_count)
    ]
    return lax.ppermute(array, ("node", "local"), perm)


def swap_core(array, node_count):
    return lax.ppermute(array, "node", [(n, n ^ 1) for n in range(node_count)])


def prepare_kernel(_, tokens_far, ids_far, weights_far, __, out, tokens, ids, weights, sems):
    pairs = ((tokens_far, tokens), (ids_far, ids), (weights_far, weights))
    copies = [
        pltpu.make_async_copy(src, dst, sems.at[i]) for i, (src, dst) in enumerate(pairs)
    ]
    for copy in copies:
        copy.start()
    for copy in copies[::-1]:
        copy.wait()
    width = tokens.shape[1]
    lane = lax.broadcasted_iota(jnp.int32, (tokens.shape[0], LANES), 1)
    coef = jnp.zeros((tokens.shape[0], LANES), F32)
    for k in range(ids.shape[1]):
        named = weights[:, k : k + 1].astype(F32)
        coef = coef + jnp.where(lane == ids[:, k : k + 1], named, 0.0)
    out[:, :width] = tokens[...]
    out[:, width:] = coef.astype(BF16)


def prepare(expert, tokens, expert_ids, route_weights, far):
    held = (tokens, expert_ids, route_weights)
    return pl.pallas_call(
        prepare_kernel,
        out_shape=VM((tokens.shape[0], tokens.shape[1] + LANES), BF16),
        in_specs=[pl.BlockSpec(memory_space=pltpu.SMEM)]
        + [pl.BlockSpec(memory_space=pltpu.HBM)] * 4,
        out_specs=pl.BlockSpec(memory_space=VM),
        scratch_shapes=[VM(x.shape, x.dtype) for x in held]
        + [pltpu.SemaphoreType.DMA((3,))],
        compiler_params=pltpu.CompilerParams(vmem_limit_bytes=2**20),
    )(expert, *[in_hbm(x) for x in (*held, far)])


def join_kernel(cuts, own, other, *outs):
    for out, a, b in zip(outs, cuts, cuts[1:]):
        rows = [own[:, a:b].astype(F32), other[:, a:b].astype(F32)]
        out[...] = jnp.concatenate(rows, axis=0).astype(BF16)


def proj_kernel(lo, hi, last, w_gate, w_up, *refs):
    parts, refs = refs[:4], refs[4:]
    gate = up = None
    if lo > 0:
        gate, up = refs[0][...], refs[1][...]
        refs = refs[2:]
    step = 896 if (hi - lo) % 896 == 0 else LANES
    for c in range(lo, hi, step):
        rows = jnp.concatenate([p[:, c - lo : c - lo + step] for p in parts], axis=0)
        g = jnp.dot(rows, w_gate[0, c : c + step, :], preferred_element_type=F32)
        u = jnp.dot(rows, w_up[0, c : c + step, :], preferred_element_type=F32)
        gate = g if gate is None else gate + g
        up = u if up is None else up + u
    if last:
        refs[0][...] = (gate / (1.0 + jnp.exp(-gate)) * up).astype(BF16)
    else:
        refs[0][...] = gate
        refs[1][...] = up


def down_kernel(lo, hi, expert, w_down, hidden, *refs):
    parts, (own_out, other_out) = refs[:-2], refs[-2:]
    half = own_out.shape[0]
    coef = jnp.concatenate([p[:, -LANES:] for p in parts], axis=0).astype(F32)
    lane = lax.broadcasted_iota(jnp.int32, coef.shape, 1)
    coef = jnp.sum(jnp.where(lane == expert[0], coef, 0.0), axis=1, keepdims=True)
    step = 512 if (hi - lo) % 512 == 0 else LANES
    h = hidden[...]
    for c in range(lo, hi, step):
        part = coef * jnp.dot(
            h, w_down[0, :, c : c + step], preferred_element_type=F32
        )
        own_out[:, c - lo : c - lo + step] = part[:half]
        other_out[:, c - lo : c - lo + step] = part[half:].astype(BF16)


def edges(width, chunks):
    tiles = width // LANES
    return [tiles * i // chunks * LANES for i in range(chunks + 1)]


def shards(tokens, expert_ids, route_weights, w_gate, w_up, w_down):
    tok_rows, width = tokens.shape
    hid = w_gate.shape[2]
    node_count = lax.axis_size("node")
    local_count = lax.axis_size("local")
    split_count = node_count * local_count // EXPERTS
    bits = local_count.bit_length() - 1
    levels = level_bits(node_count, bits)
    half = tok_rows * local_count
    rows = 2 * half
    me = lax.axis_index("node") * local_count + lax.axis_index("local")
    expert = (me // split_count).astype(jnp.int32).reshape(1)

    block = prepare(expert, tokens, expert_ids, route_weights, w_down)
    cuts = edges(width, GATHER_CHUNKS)
    wide = cuts[:-1] + [cuts[-1] + LANES]
    for k, level in enumerate(levels[:-1]):
        other = swap(block, level, local_count)
        ends = wide if k == bits - 2 else [0, width + LANES]
        blocks = call(
            functools.partial(join_kernel, ends),
            [VM((2 * block.shape[0], b - a), BF16) for a, b in zip(ends, ends[1:])],
            block,
            other,
            far=(w_down,),
            limit=1,
            flops=0,
            nbytes=200_000,
        )
        block = blocks[0]
    parts = []
    for b in blocks:
        far = swap(b, levels[-1], local_count)
        parts.append([b, far, swap_core(b, node_count), swap_core(far, node_count)])

    w_gate, w_up, w_down = in_vmem(w_gate), in_vmem(w_up), in_vmem(w_down)
    state = ()
    for i in range(GATHER_CHUNKS):
        last = i == GATHER_CHUNKS - 1
        state = call(
            functools.partial(proj_kernel, cuts[i], cuts[i + 1], last),
            [VM((rows, hid), BF16)] if last else [VM((rows, hid), F32)] * 2,
            w_gate,
            w_up,
            *parts[i],
            *state,
            limit=2,
            flops=4 * rows * hid * (cuts[i + 1] - cuts[i]),
            nbytes=4 * hid * (cuts[i + 1] - cuts[i]),
        )
    hidden = state[0]

    cuts = edges(width, RETURN_CHUNKS)
    results = []
    for a, b in zip(cuts, cuts[1:]):
        own, other = call(
            functools.partial(down_kernel, a, b),
            [VM((half, b - a), F32), VM((half, b - a), BF16)],
            w_down,
            hidden,
            *parts[-1],
            scalars=(expert,),
            limit=2,
            flops=2 * rows * hid * (b - a),
            nbytes=2 * hid * (b - a),
        )
        total = own + swap_core(other, node_count).astype(F32)
        for level in levels[::-1]:
            n = total.shape[0] // 2
            total = total[:n] + swap(total[n:].astype(BF16), level, local_count).astype(
                F32
            )
        results.append(total.astype(BF16))
    return jnp.concatenate(results, axis=1)


def solution(mesh):
    return jax.shard_map(
        shards,
        mesh=mesh,
        in_specs=(
            P(("groups", "node", "local"), None),
            P(("groups", "node", "local"), None),
            P(("groups", "node", "local"), None),
            P(("node", "local"), None, None),
            P(("node", "local"), None, None),
            P(("node", "local"), None, None),
        ),
        out_specs=P(("groups", "node", "local"), None),
        check_vma=False,
    )
```

```python
import functools

import jax
import jax.numpy as jnp
from jax import lax
from jax.experimental import pallas as pl
from jax.experimental.pallas import tpu as pltpu
from jax.sharding import PartitionSpec as P

EXPERTS = 16
LANES = 128
VM = pltpu.VMEM
F32 = jnp.float32
BF16 = jnp.bfloat16


def in_vmem(array):
    return pltpu.with_memory_space_constraint(array, VM)


def in_hbm(array):
    return pltpu.with_memory_space_constraint(array, pltpu.HBM)


def call(kernel, outs, *args, limit, flops, nbytes, scalars=(), far=()):
    def body(*refs):
        kernel(*refs[: len(scalars)], *refs[len(scalars) + len(far) :])


    return pl.pallas_call(
        body,
        out_shape=outs,
        in_specs=[pl.BlockSpec(memory_space=pltpu.SMEM)] * len(scalars)
        + [pl.BlockSpec(memory_space=pltpu.HBM)] * len(far)
        + [pl.BlockSpec(memory_space=VM)] * len(args),
        out_specs=[pl.BlockSpec(memory_space=VM)] * len(outs),
        compiler_params=pltpu.CompilerParams(vmem_limit_bytes=limit * 2**20),
        cost_estimate=pl.CostEstimate(
            flops=flops, bytes_accessed=nbytes, transcendentals=0
        ),
    )(*scalars, *[in_hbm(x) for x in far], *args)


def level_bits(node_count, bits):
    even = list(range(bits - 1, -1, -1))
    odd = even[:-2] + even[-2:][::-1]
    return [[(even, odd)[n % 2][k] for n in range(node_count)] for k in range(bits)]


def swap(array, level, local_count):
    perm = [
        (n * local_count + i, n * local_count + (i ^ (1 << bit)))
        for n, bit in enumerate(level)
        for i in range(local_count)
    ]
    return lax.ppermute(array, ("node", "local"), perm)


def swap_core(array, node_count):
    return lax.ppermute(array, "node", [(n, n ^ 1) for n in range(node_count)])


def prepare_kernel(_, tokens_far, ids_far, weights_far, __, out, tokens, ids, weights, sems):
    pairs = ((tokens_far, tokens), (ids_far, ids), (weights_far, weights))
    copies = [
        pltpu.make_async_copy(src, dst, sems.at[i]) for i, (src, dst) in enumerate(pairs)
    ]
    for copy in copies:
        copy.start()
    for copy in copies[::-1]:
        copy.wait()
    lane = lax.broadcasted_iota(jnp.int32, (tokens.shape[0], LANES), 1)
    coef = jnp.zeros((tokens.shape[0], LANES), F32)
    for k in range(ids.shape[1]):
        named = weights[:, k : k + 1].astype(F32)
        coef = coef + jnp.where(lane == ids[:, k : k + 1], named, 0.0)
    width = tokens.shape[1]
    out[:, :width] = tokens[...]
    out[:, width:] = coef.astype(BF16)


def prepare(expert, tokens, expert_ids, route_weights, far):
    held = (tokens, expert_ids, route_weights)
    return pl.pallas_call(
        prepare_kernel,
        out_shape=VM((tokens.shape[0], tokens.shape[1] + LANES), BF16),
        in_specs=[pl.BlockSpec(memory_space=pltpu.SMEM)]
        + [pl.BlockSpec(memory_space=pltpu.HBM)] * 4,
        out_specs=pl.BlockSpec(memory_space=VM),
        scratch_shapes=[VM(x.shape, x.dtype) for x in held]
        + [pltpu.SemaphoreType.DMA((3,))],
        compiler_params=pltpu.CompilerParams(vmem_limit_bytes=2**20),
        cost_estimate=pl.CostEstimate(
            flops=0, bytes_accessed=200_000, transcendentals=0
        ),
    )(expert, *[in_hbm(x) for x in (*held, far)])


def stacked(refs, columns=slice(None)):
    if any(ref.shape[0] % 16 for ref in refs):
        rows = [ref[:, columns].astype(F32) for ref in refs]
        return jnp.concatenate(rows, axis=0).astype(BF16)
    return jnp.concatenate([ref[:, columns] for ref in refs], axis=0)


def join_kernel(*refs):
    refs[-1][...] = stacked(refs[:-1])


def join(parts, far):
    rows = sum(p.shape[0] for p in parts)
    return call(
        join_kernel,
        [VM((rows, parts[0].shape[1]), BF16)],
        *parts,
        far=far,
        limit=1,
        flops=0,
        nbytes=200_000,
    )[0]


def proj_kernel(w_gate, w_up, *refs):
    parts, hidden = refs[:-1], refs[-1]
    width = w_gate.shape[1]
    step = max(n for n in range(LANES, 1025, LANES) if width % n == 0)
    gate = up = None
    for c in range(0, width, step):
        rows = stacked(parts, slice(c, c + step))
        g = jnp.dot(rows, w_gate[0, c : c + step, :], preferred_element_type=F32)
        u = jnp.dot(rows, w_up[0, c : c + step, :], preferred_element_type=F32)
        gate = g if gate is None else gate + g
        up = u if up is None else up + u
    hidden[...] = (gate / (1.0 + jnp.exp(-gate)) * up).astype(BF16)


def down_kernel(expert, w_down, hidden, *refs):
    parts, outs = refs[:-4], refs[-4:]
    low = outs[0].shape[0]
    coef = stacked(parts, slice(-LANES, None)).astype(F32)
    lane = lax.broadcasted_iota(jnp.int32, coef.shape, 1)
    coef = jnp.sum(jnp.where(lane == expert[0], coef, 0.0), axis=1, keepdims=True)
    width = w_down.shape[2]
    step = max(n for n in range(LANES, 1025, LANES) if width % n == 0)
    h = hidden[...]
    for c in range(0, width, step):
        part = coef * jnp.dot(
            h, w_down[0, :, c : c + step], preferred_element_type=F32
        )
        for i, out in enumerate(outs):
            out[:, c : c + step] = part[i * low : (i + 1) * low].astype(out.dtype)


def shards(tokens, expert_ids, route_weights, w_gate, w_up, w_down):
    tok_rows, width = tokens.shape
    hid = w_gate.shape[2]
    node_count = lax.axis_size("node")
    local_count = lax.axis_size("local")
    split_count = node_count * local_count // EXPERTS
    bits = local_count.bit_length() - 1
    dims = level_bits(node_count, bits)[::-1]
    half = tok_rows * local_count
    rows = 2 * half
    me = lax.axis_index("node") * local_count + lax.axis_index("local")
    expert = (me // split_count).astype(jnp.int32).reshape(1)

    block = prepare(expert, tokens, expert_ids, route_weights, w_down)
    mine = []
    far = swap(block, dims[-1], local_count)
    for k, half_block in enumerate((block, far)):
        for dim in dims[-2:0:-1]:
            other = swap(half_block, dim, local_count)
            half_block = join([half_block, other], (w_down,))
        other = swap(half_block, dims[0], local_count)
        if k == 0:
            mine.append(join([half_block, other], (w_down,)))
        else:
            mine += [half_block, other]
    parts = mine + [swap_core(m, node_count) for m in mine]

    w_gate, w_up, w_down = in_vmem(w_gate), in_vmem(w_up), in_vmem(w_down)
    hidden = call(
        proj_kernel,
        [VM((rows, hid), BF16)],
        w_gate,
        w_up,
        *parts,
        limit=4,
        flops=4 * rows * hid * width,
        nbytes=4 * hid * width,
    )[0]
    low = half // 2
    own_low, own_high, other_low, other_high = call(
        down_kernel,
        [VM((low, width), kind) for kind in (F32, F32, BF16, BF16)],
        w_down,
        hidden,
        *parts,
        scalars=(expert,),
        limit=4,
        flops=2 * rows * hid * width,
        nbytes=2 * hid * width,
    )
    totals = [
        own_high + swap_core(other_high, node_count).astype(F32),
        own_low + swap_core(other_low, node_count).astype(F32),
    ]
    for dim in dims[:-1]:
        n = totals[0].shape[0] // 2
        totals = [
            t[:n] + swap(t[n:].astype(BF16), dim, local_count).astype(F32)
            for t in totals
        ]
    far = swap(totals[0].astype(BF16), dims[-1], local_count)
    return (totals[1] + far.astype(F32)).astype(BF16)


def solution(mesh):
    return jax.shard_map(
        shards,
        mesh=mesh,
        in_specs=(
            P(("groups", "node", "local"), None),
            P(("groups", "node", "local"), None),
            P(("groups", "node", "local"), None),
            P(("node", "local"), None, None),
            P(("node", "local"), None, None),
            P(("node", "local"), None, None),
        ),
        out_specs=P(("groups", "node", "local"), None),
        check_vma=False,
    )
```

```python
import functools

import jax
import jax.numpy as jnp
from jax import lax
from jax.experimental import pallas as pl
from jax.experimental.pallas import tpu as pltpu
from jax.sharding import PartitionSpec as P

EXPERTS = 16
LANES = 128
VM = pltpu.VMEM
F32 = jnp.float32
BF16 = jnp.bfloat16


def in_vmem(array):
    return pltpu.with_memory_space_constraint(array, VM)


def in_hbm(array):
    return pltpu.with_memory_space_constraint(array, pltpu.HBM)


def call(kernel, outs, *args, limit, flops, nbytes, scalars=(), far=()):
    def body(*refs):
        kernel(*refs[: len(scalars)], *refs[len(scalars) + len(far) :])


    return pl.pallas_call(
        body,
        out_shape=outs,
        in_specs=[pl.BlockSpec(memory_space=pltpu.SMEM)] * len(scalars)
        + [pl.BlockSpec(memory_space=pltpu.HBM)] * len(far)
        + [pl.BlockSpec(memory_space=VM)] * len(args),
        out_specs=[pl.BlockSpec(memory_space=VM)] * len(outs),
        compiler_params=pltpu.CompilerParams(vmem_limit_bytes=limit * 2**20),
        cost_estimate=pl.CostEstimate(
            flops=flops, bytes_accessed=nbytes, transcendentals=0
        ),
    )(*scalars, *[in_hbm(x) for x in far], *args)


def level_bits(node_count, bits):
    even = list(range(bits - 1, -1, -1))
    odd = even[:-2] + even[-2:][::-1]
    return [[(even, odd)[n % 2][k] for n in range(node_count)] for k in range(bits)]


def swap_across(array, dims, mask, local_count):
    perm = []
    for n in range(len(dims[0])):
        across = sum(1 << level[n] for k, level in enumerate(dims) if mask >> k & 1)
        perm += [
            (n * local_count + i, n * local_count + (i ^ across))
            for i in range(local_count)
        ]
    return lax.ppermute(array, ("node", "local"), perm)


def swap(array, dim, local_count):
    return swap_across(array, [dim], 1, local_count)


def swap_core(array, node_count):
    return lax.ppermute(array, "node", [(n, n ^ 1) for n in range(node_count)])


def prepare_kernel(_, tokens_far, ids_far, weights_far, __, out, tokens, ids, weights, sems):
    pairs = ((tokens_far, tokens), (ids_far, ids), (weights_far, weights))
    copies = [
        pltpu.make_async_copy(src, dst, sems.at[i]) for i, (src, dst) in enumerate(pairs)
    ]
    for copy in copies:
        copy.start()
    for copy in copies[::-1]:
        copy.wait()
    lane = lax.broadcasted_iota(jnp.int32, (tokens.shape[0], LANES), 1)
    coef = jnp.zeros((tokens.shape[0], LANES), F32)
    for k in range(ids.shape[1]):
        named = weights[:, k : k + 1].astype(F32)
        coef = coef + jnp.where(lane == ids[:, k : k + 1], named, 0.0)
    width = tokens.shape[1]
    out[:, :width] = tokens[...]
    out[:, width:] = coef.astype(BF16)


def prepare(expert, tokens, expert_ids, route_weights, far):
    held = (tokens, expert_ids, route_weights)
    return pl.pallas_call(
        prepare_kernel,
        out_shape=VM((tokens.shape[0], tokens.shape[1] + LANES), BF16),
        in_specs=[pl.BlockSpec(memory_space=pltpu.SMEM)]
        + [pl.BlockSpec(memory_space=pltpu.HBM)] * 4,
        out_specs=pl.BlockSpec(memory_space=VM),
        scratch_shapes=[VM(x.shape, x.dtype) for x in held]
        + [pltpu.SemaphoreType.DMA((3,))],
        compiler_params=pltpu.CompilerParams(vmem_limit_bytes=2**20),
        cost_estimate=pl.CostEstimate(
            flops=0, bytes_accessed=200_000, transcendentals=0
        ),
    )(expert, *[in_hbm(x) for x in (*held, far)])


def stacked(refs, columns=slice(None)):
    if any(ref.shape[0] % 16 for ref in refs):
        rows = [ref[:, columns].astype(F32) for ref in refs]
        return jnp.concatenate(rows, axis=0).astype(BF16)
    return jnp.concatenate([ref[:, columns] for ref in refs], axis=0)


def join_kernel(*refs):
    refs[-1][...] = stacked(refs[:-1])


def join(parts, far):
    rows = sum(p.shape[0] for p in parts)
    return call(
        join_kernel,
        [VM((rows, parts[0].shape[1]), BF16)],
        *parts,
        far=far,
        limit=1,
        flops=0,
        nbytes=200_000,
    )[0]


def proj_kernel(w_gate, w_up, *refs):
    parts, hidden = refs[:-1], refs[-1]
    width = w_gate.shape[1]
    step = max(n for n in range(LANES, 1025, LANES) if width % n == 0)
    gate = up = None
    for c in range(0, width, step):
        rows = stacked(parts, slice(c, c + step))
        g = jnp.dot(rows, w_gate[0, c : c + step, :], preferred_element_type=F32)
        u = jnp.dot(rows, w_up[0, c : c + step, :], preferred_element_type=F32)
        gate = g if gate is None else gate + g
        up = u if up is None else up + u
    hidden[...] = (gate / (1.0 + jnp.exp(-gate)) * up).astype(BF16)


def down_kernel(expert, w_down, hidden, *refs):
    parts, outs = refs[:-4], refs[-4:]
    low = outs[0].shape[0]
    coef = stacked(parts, slice(-LANES, None)).astype(F32)
    lane = lax.broadcasted_iota(jnp.int32, coef.shape, 1)
    coef = jnp.sum(jnp.where(lane == expert[0], coef, 0.0), axis=1, keepdims=True)
    width = w_down.shape[2]
    step = max(n for n in range(LANES, 1025, LANES) if width % n == 0)
    h = hidden[...]
    for c in range(0, width, step):
        part = coef * jnp.dot(
            h, w_down[0, :, c : c + step], preferred_element_type=F32
        )
        for i, out in enumerate(outs):
            out[:, c : c + step] = part[i * low : (i + 1) * low].astype(out.dtype)


def shards(tokens, expert_ids, route_weights, w_gate, w_up, w_down):
    tok_rows, width = tokens.shape
    hid = w_gate.shape[2]
    node_count = lax.axis_size("node")
    local_count = lax.axis_size("local")
    split_count = node_count * local_count // EXPERTS
    bits = local_count.bit_length() - 1
    dims = level_bits(node_count, bits)[::-1]
    half = tok_rows * local_count
    rows = 2 * half
    me = lax.axis_index("node") * local_count + lax.axis_index("local")
    expert = (me // split_count).astype(jnp.int32).reshape(1)

    side = local_count // 2
    masks = [
        sum(1 << k for k in range(bits - 1) if i >> (bits - 2 - k) & 1)
        for i in range(side)
    ]
    near = prepare(expert, tokens, expert_ids, route_weights, w_down)
    far = [swap(near, dims[-1], local_count)]
    far += [swap_across(far[0], dims, m, local_count) for m in masks[1:]]
    for dim in dims[-2::-1]:
        near = join([near, swap(near, dim, local_count)], (w_down,))
    mine = [near, join(far, (w_down,))]
    parts = mine + [swap_core(m, node_count) for m in mine]

    w_gate, w_up, w_down = in_vmem(w_gate), in_vmem(w_up), in_vmem(w_down)
    hidden = call(
        proj_kernel,
        [VM((rows, hid), BF16)],
        w_gate,
        w_up,
        *parts,
        limit=4,
        flops=4 * rows * hid * width,
        nbytes=4 * hid * width,
    )[0]
    low = half // 2
    own_low, own_high, other_low, other_high = call(
        down_kernel,
        [VM((low, width), kind) for kind in (F32, F32, BF16, BF16)],
        w_down,
        hidden,
        *parts,
        scalars=(expert,),
        limit=4,
        flops=2 * rows * hid * width,
        nbytes=2 * hid * width,
    )
    def halve(total, dim):
        n = total.shape[0] // 2
        return total[:n] + swap(total[n:].astype(BF16), dim, local_count).astype(F32)

    def gather_side(rows):
        total = rows[:tok_rows]
        for i in range(1, local_count // 2):
            part = rows[i * tok_rows : (i + 1) * tok_rows].astype(BF16)
            mask = sum(1 << k for k in range(bits - 1) if i >> (bits - 2 - k) & 1)
            total = total + swap_across(part, dims, mask, local_count).astype(F32)
        return total

    far = own_high + swap_core(other_high, node_count).astype(F32)
    near = own_low + swap_core(other_low, node_count).astype(F32)
    far = gather_side(far)
    for dim in dims[:-1]:
        near = halve(near, dim)
    far = swap(far.astype(BF16), dims[-1], local_count)
    return (near + far.astype(F32)).astype(BF16)


def solution(mesh):
    return jax.shard_map(
        shards,
        mesh=mesh,
        in_specs=(
            P(("groups", "node", "local"), None),
            P(("groups", "node", "local"), None),
            P(("groups", "node", "local"), None),
            P(("node", "local"), None, None),
            P(("node", "local"), None, None),
            P(("node", "local"), None, None),
        ),
        out_specs=P(("groups", "node", "local"), None),
        check_vma=False,
    )
```

```python
import functools

import jax
import jax.numpy as jnp
from jax import lax
from jax.experimental import pallas as pl
from jax.experimental.pallas import tpu as pltpu
from jax.sharding import PartitionSpec as P

EXPERTS = 16
LANES = 128
VM = pltpu.VMEM
F32 = jnp.float32
BF16 = jnp.bfloat16


def in_vmem(array):
    return pltpu.with_memory_space_constraint(array, VM)


def in_hbm(array):
    return pltpu.with_memory_space_constraint(array, pltpu.HBM)


def call(kernel, outs, *args, limit, flops, nbytes, scalars=(), far=(), after=()):
    def body(*refs):
        kernel(*refs[: len(scalars)], *refs[len(scalars) + len(far) + len(after) :])


    return pl.pallas_call(
        body,
        out_shape=outs,
        in_specs=[pl.BlockSpec(memory_space=pltpu.SMEM)] * len(scalars)
        + [pl.BlockSpec(memory_space=pltpu.HBM)] * len(far)
        + [pl.BlockSpec(memory_space=pl.ANY)] * len(after)
        + [pl.BlockSpec(memory_space=VM)] * len(args),
        out_specs=[pl.BlockSpec(memory_space=VM)] * len(outs),
        compiler_params=pltpu.CompilerParams(vmem_limit_bytes=limit * 2**20),
        cost_estimate=pl.CostEstimate(
            flops=flops, bytes_accessed=nbytes, transcendentals=0
        ),
    )(*scalars, *[in_hbm(x) for x in far], *after, *args)


def level_bits(node_count, bits):
    even = list(range(bits - 1, -1, -1))
    odd = even[:-2] + even[-2:][::-1]
    return [[(even, odd)[n % 2][k] for n in range(node_count)] for k in range(bits)]


def swap_across(array, dims, mask, local_count):
    perm = []
    for n in range(len(dims[0])):
        across = sum(1 << level[n] for k, level in enumerate(dims) if mask >> k & 1)
        perm += [
            (n * local_count + i, n * local_count + (i ^ across))
            for i in range(local_count)
        ]
    return lax.ppermute(array, ("node", "local"), perm)


def swap(array, dim, local_count):
    return swap_across(array, [dim], 1, local_count)


def swap_core(array, node_count):
    return lax.ppermute(array, "node", [(n, n ^ 1) for n in range(node_count)])


def prepare_kernel(_, tokens_far, ids_far, weights_far, __, out, tokens, ids, weights, sems):
    pairs = ((tokens_far, tokens), (ids_far, ids), (weights_far, weights))
    copies = [
        pltpu.make_async_copy(src, dst, sems.at[i]) for i, (src, dst) in enumerate(pairs)
    ]
    for copy in copies:
        copy.start()
    for copy in copies[::-1]:
        copy.wait()
    lane = lax.broadcasted_iota(jnp.int32, (tokens.shape[0], LANES), 1)
    coef = jnp.zeros((tokens.shape[0], LANES), F32)
    for k in range(ids.shape[1]):
        named = weights[:, k : k + 1].astype(F32)
        coef = coef + jnp.where(lane == ids[:, k : k + 1], named, 0.0)
    width = tokens.shape[1]
    out[:, :width] = tokens[...]
    out[:, width:] = coef.astype(BF16)


def prepare(expert, tokens, expert_ids, route_weights, far):
    held = (tokens, expert_ids, route_weights)
    return pl.pallas_call(
        prepare_kernel,
        out_shape=VM((tokens.shape[0], tokens.shape[1] + LANES), BF16),
        in_specs=[pl.BlockSpec(memory_space=pltpu.SMEM)]
        + [pl.BlockSpec(memory_space=pltpu.HBM)] * 4,
        out_specs=pl.BlockSpec(memory_space=VM),
        scratch_shapes=[VM(x.shape, x.dtype) for x in held]
        + [pltpu.SemaphoreType.DMA((3,))],
        compiler_params=pltpu.CompilerParams(vmem_limit_bytes=2**20),
        cost_estimate=pl.CostEstimate(
            flops=0, bytes_accessed=200_000, transcendentals=0
        ),
    )(expert, *[in_hbm(x) for x in (*held, far)])


def stacked(refs, columns=slice(None)):
    if any(ref.shape[0] % 16 for ref in refs):
        rows = [ref[:, columns].astype(F32) for ref in refs]
        return jnp.concatenate(rows, axis=0).astype(BF16)
    return jnp.concatenate([ref[:, columns] for ref in refs], axis=0)


def join_kernel(*refs):
    refs[-1][...] = stacked(refs[:-1])


def join(parts, far, after=()):
    rows = sum(p.shape[0] for p in parts)
    return call(
        join_kernel,
        [VM((rows, parts[0].shape[1]), BF16)],
        *parts,
        far=far,
        after=after,
        limit=1,
        flops=0,
        nbytes=200_000,
    )[0]


def proj_kernel(w_gate, w_up, *refs):
    parts, hidden = refs[:-1], refs[-1]
    width = w_gate.shape[1]
    step = max(n for n in range(LANES, 1025, LANES) if width % n == 0)
    gate = up = None
    for c in range(0, width, step):
        rows = stacked(parts, slice(c, c + step))
        g = jnp.dot(rows, w_gate[0, c : c + step, :], preferred_element_type=F32)
        u = jnp.dot(rows, w_up[0, c : c + step, :], preferred_element_type=F32)
        gate = g if gate is None else gate + g
        up = u if up is None else up + u
    hidden[...] = (gate / (1.0 + jnp.exp(-gate)) * up).astype(BF16)


def down_kernel(expert, w_down, hidden, *refs):
    parts, outs = refs[:-4], refs[-4:]
    low = outs[0].shape[0]
    coef = stacked(parts, slice(-LANES, None)).astype(F32)
    lane = lax.broadcasted_iota(jnp.int32, coef.shape, 1)
    coef = jnp.sum(jnp.where(lane == expert[0], coef, 0.0), axis=1, keepdims=True)
    width = w_down.shape[2]
    step = max(n for n in range(LANES, 1025, LANES) if width % n == 0)
    h = hidden[...]
    for c in range(0, width, step):
        part = coef * jnp.dot(
            h, w_down[0, :, c : c + step], preferred_element_type=F32
        )
        for i, out in enumerate(outs):
            out[:, c : c + step] = part[i * low : (i + 1) * low].astype(out.dtype)


def shards(tokens, expert_ids, route_weights, w_gate, w_up, w_down):
    tok_rows, width = tokens.shape
    hid = w_gate.shape[2]
    node_count = lax.axis_size("node")
    local_count = lax.axis_size("local")
    split_count = node_count * local_count // EXPERTS
    bits = local_count.bit_length() - 1
    dims = level_bits(node_count, bits)[::-1]
    half = tok_rows * local_count
    rows = 2 * half
    me = lax.axis_index("node") * local_count + lax.axis_index("local")
    expert = (me // split_count).astype(jnp.int32).reshape(1)

    side = local_count // 2
    masks = [
        sum(1 << k for k in range(bits - 1) if i >> (bits - 2 - k) & 1)
        for i in range(side)
    ]
    block = prepare(expert, tokens, expert_ids, route_weights, w_down)
    far = [swap(block, dims[-1], local_count)]
    near = [block] + [swap_across(block, dims, m, local_count) for m in masks[1:]]
    far += [swap_across(far[0], dims, m, local_count) for m in masks[1:]]
    near = join(near, (w_down,), ())
    far = join(far, (w_down,))
    mine = [near, far]
    parts = mine + [swap_core(m, node_count) for m in mine]

    w_gate, w_up, w_down = in_vmem(w_gate), in_vmem(w_up), in_vmem(w_down)
    hidden = call(
        proj_kernel,
        [VM((rows, hid), BF16)],
        w_gate,
        w_up,
        *parts,
        limit=4,
        flops=4 * rows * hid * width,
        nbytes=4 * hid * width,
    )[0]
    low = half // 2
    own_low, own_high, other_low, other_high = call(
        down_kernel,
        [VM((low, width), kind) for kind in (F32, F32, BF16, BF16)],
        w_down,
        hidden,
        *parts,
        scalars=(expert,),
        limit=4,
        flops=2 * rows * hid * width,
        nbytes=2 * hid * width,
    )
    def halve(total, dim):
        n = total.shape[0] // 2
        return total[:n] + swap(total[n:].astype(BF16), dim, local_count).astype(F32)

    def gather_side(rows):
        total = rows[:tok_rows]
        for i in range(1, local_count // 2):
            part = rows[i * tok_rows : (i + 1) * tok_rows].astype(BF16)
            mask = sum(1 << k for k in range(bits - 1) if i >> (bits - 2 - k) & 1)
            total = total + swap_across(part, dims, mask, local_count).astype(F32)
        return total

    far = own_high + swap_core(other_high, node_count).astype(F32)
    near = own_low + swap_core(other_low, node_count).astype(F32)
    far = gather_side(far)
    for dim in dims[:-1]:
        near = halve(near, dim)
    far = swap(far.astype(BF16), dims[-1], local_count)
    return (near + far.astype(F32)).astype(BF16)


def solution(mesh):
    return jax.shard_map(
        shards,
        mesh=mesh,
        in_specs=(
            P(("groups", "node", "local"), None),
            P(("groups", "node", "local"), None),
            P(("groups", "node", "local"), None),
            P(("node", "local"), None, None),
            P(("node", "local"), None, None),
            P(("node", "local"), None, None),
        ),
        out_specs=P(("groups", "node", "local"), None),
        check_vma=False,
    )
```

```python
import functools

import jax
import jax.numpy as jnp
from jax import lax
from jax.experimental import pallas as pl
from jax.experimental.pallas import tpu as pltpu
from jax.sharding import PartitionSpec as P

EXPERTS = 16
LANES = 128
VM = pltpu.VMEM
F32 = jnp.float32
BF16 = jnp.bfloat16


def in_vmem(array):
    return pltpu.with_memory_space_constraint(array, VM)


def in_hbm(array):
    return pltpu.with_memory_space_constraint(array, pltpu.HBM)


def call(kernel, outs, *args, limit, flops, nbytes, scalars=(), far=(), after=()):
    def body(*refs):
        kernel(*refs[: len(scalars)], *refs[len(scalars) + len(far) + len(after) :])


    return pl.pallas_call(
        body,
        out_shape=outs,
        in_specs=[pl.BlockSpec(memory_space=pltpu.SMEM)] * len(scalars)
        + [pl.BlockSpec(memory_space=pltpu.HBM)] * len(far)
        + [pl.BlockSpec(memory_space=pl.ANY)] * len(after)
        + [pl.BlockSpec(memory_space=VM)] * len(args),
        out_specs=[pl.BlockSpec(memory_space=VM)] * len(outs),
        compiler_params=pltpu.CompilerParams(vmem_limit_bytes=limit * 2**20),
        cost_estimate=pl.CostEstimate(
            flops=flops, bytes_accessed=nbytes, transcendentals=0
        ),
    )(*scalars, *[in_hbm(x) for x in far], *after, *args)


def level_bits(node_count, bits):
    even = list(range(bits - 1, -1, -1))
    odd = even[:-2] + even[-2:][::-1]
    return [[(even, odd)[n % 2][k] for n in range(node_count)] for k in range(bits)]


def swap_across(array, dims, mask, local_count):
    perm = []
    for n in range(len(dims[0])):
        across = sum(1 << level[n] for k, level in enumerate(dims) if mask >> k & 1)
        perm += [
            (n * local_count + i, n * local_count + (i ^ across))
            for i in range(local_count)
        ]
    return lax.ppermute(array, ("node", "local"), perm)


def swap(array, dim, local_count):
    return swap_across(array, [dim], 1, local_count)


def swap_core(array, node_count):
    return lax.ppermute(array, "node", [(n, n ^ 1) for n in range(node_count)])


def prepare_kernel(_, tokens_far, ids_far, weights_far, __, out, tokens, ids, weights, sems):
    pairs = ((tokens_far, tokens), (ids_far, ids), (weights_far, weights))
    copies = [
        pltpu.make_async_copy(src, dst, sems.at[i]) for i, (src, dst) in enumerate(pairs)
    ]
    for copy in copies:
        copy.start()
    for copy in copies[::-1]:
        copy.wait()
    lane = lax.broadcasted_iota(jnp.int32, (tokens.shape[0], LANES), 1)
    coef = jnp.zeros((tokens.shape[0], LANES), F32)
    for k in range(ids.shape[1]):
        named = weights[:, k : k + 1].astype(F32)
        coef = coef + jnp.where(lane == ids[:, k : k + 1], named, 0.0)
    width = tokens.shape[1]
    out[:, :width] = tokens[...]
    out[:, width:] = coef.astype(BF16)


def prepare(expert, tokens, expert_ids, route_weights, far):
    held = (tokens, expert_ids, route_weights)
    return pl.pallas_call(
        prepare_kernel,
        out_shape=VM((tokens.shape[0], tokens.shape[1] + LANES), BF16),
        in_specs=[pl.BlockSpec(memory_space=pltpu.SMEM)]
        + [pl.BlockSpec(memory_space=pltpu.HBM)] * 4,
        out_specs=pl.BlockSpec(memory_space=VM),
        scratch_shapes=[VM(x.shape, x.dtype) for x in held]
        + [pltpu.SemaphoreType.DMA((3,))],
        compiler_params=pltpu.CompilerParams(vmem_limit_bytes=2**20),
        cost_estimate=pl.CostEstimate(
            flops=0, bytes_accessed=200_000, transcendentals=0
        ),
    )(expert, *[in_hbm(x) for x in (*held, far)])


def stacked(refs, columns=slice(None)):
    if any(ref.shape[0] % 16 for ref in refs):
        rows = [ref[:, columns].astype(F32) for ref in refs]
        return jnp.concatenate(rows, axis=0).astype(BF16)
    return jnp.concatenate([ref[:, columns] for ref in refs], axis=0)


def join_kernel(*refs):
    refs[-1][...] = stacked(refs[:-1])


def join(parts, far, after=()):
    rows = sum(p.shape[0] for p in parts)
    return call(
        join_kernel,
        [VM((rows, parts[0].shape[1]), BF16)],
        *parts,
        far=far,
        after=after,
        limit=1,
        flops=0,
        nbytes=200_000,
    )[0]


def proj_kernel(w_gate, w_up, *refs):
    parts, hidden = refs[:-1], refs[-1]
    width = w_gate.shape[1]
    step = max(n for n in range(LANES, 1025, LANES) if width % n == 0)
    gate = up = None
    for c in range(0, width, step):
        rows = stacked(parts, slice(c, c + step))
        g = jnp.dot(rows, w_gate[0, c : c + step, :], preferred_element_type=F32)
        u = jnp.dot(rows, w_up[0, c : c + step, :], preferred_element_type=F32)
        gate = g if gate is None else gate + g
        up = u if up is None else up + u
    hidden[...] = (gate / (1.0 + jnp.exp(-gate)) * up).astype(BF16)


def down_kernel(expert, w_down, hidden, *refs):
    parts, outs = refs[:-4], refs[-4:]
    low = outs[0].shape[0]
    coef = stacked(parts, slice(-LANES, None)).astype(F32)
    lane = lax.broadcasted_iota(jnp.int32, coef.shape, 1)
    coef = jnp.sum(jnp.where(lane == expert[0], coef, 0.0), axis=1, keepdims=True)
    width = w_down.shape[2]
    step = max(n for n in range(LANES, 1025, LANES) if width % n == 0)
    h = hidden[...]
    for c in range(0, width, step):
        part = coef * jnp.dot(
            h, w_down[0, :, c : c + step], preferred_element_type=F32
        )
        for i, out in enumerate(outs):
            out[:, c : c + step] = part[i * low : (i + 1) * low].astype(out.dtype)


def shards(tokens, expert_ids, route_weights, w_gate, w_up, w_down):
    tok_rows, width = tokens.shape
    hid = w_gate.shape[2]
    node_count = lax.axis_size("node")
    local_count = lax.axis_size("local")
    split_count = node_count * local_count // EXPERTS
    bits = local_count.bit_length() - 1
    dims = level_bits(node_count, bits)[::-1]
    half = tok_rows * local_count
    rows = 2 * half
    me = lax.axis_index("node") * local_count + lax.axis_index("local")
    expert = (me // split_count).astype(jnp.int32).reshape(1)

    side = local_count // 2
    masks = [
        sum(1 << k for k in range(bits - 1) if i >> (bits - 2 - k) & 1)
        for i in range(side)
    ]
    block = prepare(expert, tokens, expert_ids, route_weights, w_down)
    far = [swap(block, dims[-1], local_count)]
    near = [block] + [swap_across(block, dims, m, local_count) for m in range(1, side)]
    far += [swap_across(far[0], dims, m, local_count) for m in masks[1:]]
    near = join(near, (w_down,), ())
    far = join(far, (w_down,))
    mine = [near, far]
    parts = mine + [swap_core(m, node_count) for m in mine]

    w_gate, w_up, w_down = in_vmem(w_gate), in_vmem(w_up), in_vmem(w_down)
    hidden = call(
        proj_kernel,
        [VM((rows, hid), BF16)],
        w_gate,
        w_up,
        *parts,
        limit=4,
        flops=4 * rows * hid * width,
        nbytes=4 * hid * width,
    )[0]
    low = half // 2
    own_low, own_high, other_low, other_high = call(
        down_kernel,
        [VM((low, width), kind) for kind in (F32, F32, BF16, BF16)],
        w_down,
        hidden,
        *parts,
        scalars=(expert,),
        limit=4,
        flops=2 * rows * hid * width,
        nbytes=2 * hid * width,
    )
    def halve(total, dim):
        n = total.shape[0] // 2
        return total[:n] + swap(total[n:].astype(BF16), dim, local_count).astype(F32)

    def gather_side(rows):
        total = rows[:tok_rows]
        for i in range(local_count // 2 - 1, 0, -1):
            part = rows[i * tok_rows : (i + 1) * tok_rows].astype(BF16)
            mask = sum(1 << k for k in range(bits - 1) if i >> (bits - 2 - k) & 1)
            total = total + swap_across(part, dims, mask, local_count).astype(F32)
        return total

    far = own_high + swap_core(other_high, node_count).astype(F32)
    near = own_low + swap_core(other_low, node_count).astype(F32)
    far = gather_side(far)
    for dim in dims[-2::-1]:
        near = halve(near, dim)
    far = swap(far.astype(BF16), dims[-1], local_count)
    return (near + far.astype(F32)).astype(BF16)


def solution(mesh):
    return jax.shard_map(
        shards,
        mesh=mesh,
        in_specs=(
            P(("groups", "node", "local"), None),
            P(("groups", "node", "local"), None),
            P(("groups", "node", "local"), None),
            P(("node", "local"), None, None),
            P(("node", "local"), None, None),
            P(("node", "local"), None, None),
        ),
        out_specs=P(("groups", "node", "local"), None),
        check_vma=False,
    )
```

```python
import functools

import jax
import jax.numpy as jnp
from jax import lax
from jax.experimental import pallas as pl
from jax.experimental.pallas import tpu as pltpu
from jax.sharding import PartitionSpec as P

EXPERTS = 16
LANES = 128
VM = pltpu.VMEM
F32 = jnp.float32
BF16 = jnp.bfloat16


def in_vmem(array):
    return pltpu.with_memory_space_constraint(array, VM)


def in_hbm(array):
    return pltpu.with_memory_space_constraint(array, pltpu.HBM)


def call(kernel, outs, *args, limit, flops, nbytes, scalars=(), far=(), after=()):
    def body(*refs):
        kernel(*refs[: len(scalars)], *refs[len(scalars) + len(far) + len(after) :])


    return pl.pallas_call(
        body,
        out_shape=outs,
        in_specs=[pl.BlockSpec(memory_space=pltpu.SMEM)] * len(scalars)
        + [pl.BlockSpec(memory_space=pltpu.HBM)] * len(far)
        + [pl.BlockSpec(memory_space=pl.ANY)] * len(after)
        + [pl.BlockSpec(memory_space=VM)] * len(args),
        out_specs=[pl.BlockSpec(memory_space=VM)] * len(outs),
        compiler_params=pltpu.CompilerParams(vmem_limit_bytes=limit * 2**20),
        cost_estimate=pl.CostEstimate(
            flops=flops, bytes_accessed=nbytes, transcendentals=0
        ),
    )(*scalars, *[in_hbm(x) for x in far], *after, *args)


def level_bits(node_count, bits):
    even = list(range(bits - 1, -1, -1))
    odd = even[:-2] + even[-2:][::-1]
    return [[(even, odd)[n % 2][k] for n in range(node_count)] for k in range(bits)]


def swap_across(array, dims, mask, local_count):
    perm = []
    for n in range(len(dims[0])):
        across = sum(1 << level[n] for k, level in enumerate(dims) if mask >> k & 1)
        perm += [
            (n * local_count + i, n * local_count + (i ^ across))
            for i in range(local_count)
        ]
    return lax.ppermute(array, ("node", "local"), perm)


def swap(array, dim, local_count):
    return swap_across(array, [dim], 1, local_count)


def swap_core(array, node_count):
    return lax.ppermute(array, "node", [(n, n ^ 1) for n in range(node_count)])


def prepare_kernel(_, tokens_far, ids_far, weights_far, __, out, tokens, ids, weights, sems):
    pairs = ((tokens_far, tokens), (ids_far, ids), (weights_far, weights))
    copies = [
        pltpu.make_async_copy(src, dst, sems.at[i]) for i, (src, dst) in enumerate(pairs)
    ]
    for copy in copies:
        copy.start()
    for copy in copies[::-1]:
        copy.wait()
    lane = lax.broadcasted_iota(jnp.int32, (tokens.shape[0], LANES), 1)
    coef = jnp.zeros((tokens.shape[0], LANES), F32)
    for k in range(ids.shape[1]):
        named = weights[:, k : k + 1].astype(F32)
        coef = coef + jnp.where(lane == ids[:, k : k + 1], named, 0.0)
    width = tokens.shape[1]
    out[:, :width] = tokens[...]
    out[:, width:] = coef.astype(BF16)


def prepare(expert, tokens, expert_ids, route_weights, far):
    held = (tokens, expert_ids, route_weights)
    return pl.pallas_call(
        prepare_kernel,
        out_shape=VM((tokens.shape[0], tokens.shape[1] + LANES), BF16),
        in_specs=[pl.BlockSpec(memory_space=pltpu.SMEM)]
        + [pl.BlockSpec(memory_space=pltpu.HBM)] * 4,
        out_specs=pl.BlockSpec(memory_space=VM),
        scratch_shapes=[VM(x.shape, x.dtype) for x in held]
        + [pltpu.SemaphoreType.DMA((3,))],
        compiler_params=pltpu.CompilerParams(vmem_limit_bytes=2**20),
        cost_estimate=pl.CostEstimate(
            flops=0, bytes_accessed=200_000, transcendentals=0
        ),
    )(expert, *[in_hbm(x) for x in (*held, far)])


def stacked(refs, columns=slice(None)):
    if any(ref.shape[0] % 16 for ref in refs):
        rows = [ref[:, columns].astype(F32) for ref in refs]
        return jnp.concatenate(rows, axis=0).astype(BF16)
    return jnp.concatenate([ref[:, columns] for ref in refs], axis=0)


def join_kernel(*refs):
    refs[-1][...] = stacked(refs[:-1])


def join(parts, far, after=()):
    rows = sum(p.shape[0] for p in parts)
    return call(
        join_kernel,
        [VM((rows, parts[0].shape[1]), BF16)],
        *parts,
        far=far,
        after=after,
        limit=1,
        flops=0,
        nbytes=200_000,
    )[0]


def proj_kernel(w_gate, w_up, *refs):
    parts, hidden = refs[:-1], refs[-1]
    width = w_gate.shape[1]
    step = max(n for n in range(LANES, 1025, LANES) if width % n == 0)
    gate = up = None
    for c in range(0, width, step):
        rows = stacked(parts, slice(c, c + step))
        g = jnp.dot(rows, w_gate[0, c : c + step, :], preferred_element_type=F32)
        u = jnp.dot(rows, w_up[0, c : c + step, :], preferred_element_type=F32)
        gate = g if gate is None else gate + g
        up = u if up is None else up + u
    hidden[...] = (gate / (1.0 + jnp.exp(-gate)) * up).astype(BF16)


def down_kernel(expert, w_down, hidden, *refs):
    parts, outs = refs[:-4], refs[-4:]
    low = outs[0].shape[0]
    coef = stacked(parts, slice(-LANES, None)).astype(F32)
    lane = lax.broadcasted_iota(jnp.int32, coef.shape, 1)
    coef = jnp.sum(jnp.where(lane == expert[0], coef, 0.0), axis=1, keepdims=True)
    width = w_down.shape[2]
    step = max(n for n in range(LANES, 1025, LANES) if width % n == 0)
    h = hidden[...]
    for c in range(0, width, step):
        part = coef * jnp.dot(
            h, w_down[0, :, c : c + step], preferred_element_type=F32
        )
        for i, out in enumerate(outs):
            out[:, c : c + step] = part[i * low : (i + 1) * low].astype(out.dtype)


def shards(tokens, expert_ids, route_weights, w_gate, w_up, w_down):
    tok_rows, width = tokens.shape
    hid = w_gate.shape[2]
    node_count = lax.axis_size("node")
    local_count = lax.axis_size("local")
    split_count = node_count * local_count // EXPERTS
    bits = local_count.bit_length() - 1
    dims = level_bits(node_count, bits)[::-1]
    half = tok_rows * local_count
    rows = 2 * half
    me = lax.axis_index("node") * local_count + lax.axis_index("local")
    expert = (me // split_count).astype(jnp.int32).reshape(1)

    side = local_count // 2
    masks = [
        sum(1 << k for k in range(bits - 1) if i >> (bits - 2 - k) & 1)
        for i in range(side)
    ]
    block = prepare(expert, tokens, expert_ids, route_weights, w_down)
    far = [swap(block, dims[-1], local_count)]
    near = [block] + [swap_across(block, dims, m, local_count) for m in range(1, side)]
    far += [swap_across(far[0], dims, m, local_count) for m in masks[1:]]
    near = join(near, (w_down,), ())
    far = join(far, (w_down,))
    mine = [near, far]
    parts = mine + [swap_core(m, node_count) for m in mine]

    w_gate, w_up, w_down = in_vmem(w_gate), in_vmem(w_up), in_vmem(w_down)
    hidden = call(
        proj_kernel,
        [VM((rows, hid), BF16)],
        w_gate,
        w_up,
        *parts,
        limit=4,
        flops=4 * rows * hid * width,
        nbytes=4 * hid * width,
    )[0]
    low = half // 2
    own_low, own_high, other_low, other_high = call(
        down_kernel,
        [VM((low, width), kind) for kind in (F32, F32, BF16, BF16)],
        w_down,
        hidden,
        *parts,
        scalars=(expert,),
        limit=4,
        flops=2 * rows * hid * width,
        nbytes=2 * hid * width,
    )
    def halve(total, dim):
        n = total.shape[0] // 2
        return total[:n] + swap(total[n:].astype(BF16), dim, local_count).astype(F32)

    def gather_side(rows):
        total = rows[:tok_rows]
        for i in [*range(2, local_count // 2), 1]:
            part = rows[i * tok_rows : (i + 1) * tok_rows].astype(BF16)
            mask = sum(1 << k for k in range(bits - 1) if i >> (bits - 2 - k) & 1)
            total = total + swap_across(part, dims, mask, local_count).astype(F32)
        return total

    far = own_high + swap_core(other_high, node_count).astype(F32)
    near = own_low + swap_core(other_low, node_count).astype(F32)
    far = gather_side(far)
    for dim in dims[-2::-1]:
        near = halve(near, dim)
    far = swap(far.astype(BF16), dims[-1], local_count)
    return (near + far.astype(F32)).astype(BF16)


def solution(mesh):
    return jax.shard_map(
        shards,
        mesh=mesh,
        in_specs=(
            P(("groups", "node", "local"), None),
            P(("groups", "node", "local"), None),
            P(("groups", "node", "local"), None),
            P(("node", "local"), None, None),
            P(("node", "local"), None, None),
            P(("node", "local"), None, None),
        ),
        out_specs=P(("groups", "node", "local"), None),
        check_vma=False,
    )
```

```python
import functools

import jax
import jax.numpy as jnp
from jax import lax
from jax.experimental import pallas as pl
from jax.experimental.pallas import tpu as pltpu
from jax.sharding import PartitionSpec as P

EXPERTS = 16
LANES = 128
VM = pltpu.VMEM
F32 = jnp.float32
BF16 = jnp.bfloat16


def in_vmem(array):
    return pltpu.with_memory_space_constraint(array, VM)


def in_hbm(array):
    return pltpu.with_memory_space_constraint(array, pltpu.HBM)


def call(kernel, outs, *args, limit, flops, nbytes, scalars=(), far=(), after=()):
    def body(*refs):
        kernel(*refs[: len(scalars)], *refs[len(scalars) + len(far) + len(after) :])


    return pl.pallas_call(
        body,
        out_shape=outs,
        in_specs=[pl.BlockSpec(memory_space=pltpu.SMEM)] * len(scalars)
        + [pl.BlockSpec(memory_space=pltpu.HBM)] * len(far)
        + [pl.BlockSpec(memory_space=pl.ANY)] * len(after)
        + [pl.BlockSpec(memory_space=VM)] * len(args),
        out_specs=[pl.BlockSpec(memory_space=VM)] * len(outs),
        compiler_params=pltpu.CompilerParams(vmem_limit_bytes=limit * 2**20),
        cost_estimate=pl.CostEstimate(
            flops=flops, bytes_accessed=nbytes, transcendentals=0
        ),
    )(*scalars, *[in_hbm(x) for x in far], *after, *args)


def level_bits(node_count, bits):
    even = list(range(bits - 1, -1, -1))
    odd = even[:-2] + even[-2:][::-1]
    return [[(even, odd)[n % 2][k] for n in range(node_count)] for k in range(bits)]


def swap_across(array, dims, mask, local_count):
    perm = []
    for n in range(len(dims[0])):
        across = sum(1 << level[n] for k, level in enumerate(dims) if mask >> k & 1)
        perm += [
            (n * local_count + i, n * local_count + (i ^ across))
            for i in range(local_count)
        ]
    return lax.ppermute(array, ("node", "local"), perm)


def swap(array, dim, local_count):
    return swap_across(array, [dim], 1, local_count)


def swap_core(array, node_count):
    return lax.ppermute(array, "node", [(n, n ^ 1) for n in range(node_count)])


def prepare_kernel(_, tokens_far, ids_far, weights_far, __, out, tokens, ids, weights, sems):
    pairs = ((tokens_far, tokens), (ids_far, ids), (weights_far, weights))
    copies = [
        pltpu.make_async_copy(src, dst, sems.at[i]) for i, (src, dst) in enumerate(pairs)
    ]
    for copy in copies:
        copy.start()
    for copy in copies[::-1]:
        copy.wait()
    lane = lax.broadcasted_iota(jnp.int32, (tokens.shape[0], LANES), 1)
    coef = jnp.zeros((tokens.shape[0], LANES), F32)
    for k in range(ids.shape[1]):
        named = weights[:, k : k + 1].astype(F32)
        coef = coef + jnp.where(lane == ids[:, k : k + 1], named, 0.0)
    width = tokens.shape[1]
    out[:, :width] = tokens[...]
    out[:, width:] = coef.astype(BF16)


def prepare(expert, tokens, expert_ids, route_weights, far):
    held = (tokens, expert_ids, route_weights)
    return pl.pallas_call(
        prepare_kernel,
        out_shape=VM((tokens.shape[0], tokens.shape[1] + LANES), BF16),
        in_specs=[pl.BlockSpec(memory_space=pltpu.SMEM)]
        + [pl.BlockSpec(memory_space=pltpu.HBM)] * 4,
        out_specs=pl.BlockSpec(memory_space=VM),
        scratch_shapes=[VM(x.shape, x.dtype) for x in held]
        + [pltpu.SemaphoreType.DMA((3,))],
        compiler_params=pltpu.CompilerParams(vmem_limit_bytes=2**20),
        cost_estimate=pl.CostEstimate(
            flops=0, bytes_accessed=200_000, transcendentals=0
        ),
    )(expert, *[in_hbm(x) for x in (*held, far)])


def stacked(refs, columns=slice(None)):
    if any(ref.shape[0] % 16 for ref in refs):
        rows = [ref[:, columns].astype(F32) for ref in refs]
        return jnp.concatenate(rows, axis=0).astype(BF16)
    return jnp.concatenate([ref[:, columns] for ref in refs], axis=0)


def join_kernel(*refs):
    refs[-1][...] = stacked(refs[:-1])


def join(parts, far, after=()):
    rows = sum(p.shape[0] for p in parts)
    return call(
        join_kernel,
        [VM((rows, parts[0].shape[1]), BF16)],
        *parts,
        far=far,
        after=after,
        limit=1,
        flops=0,
        nbytes=200_000,
    )[0]


def proj_kernel(w_gate, w_up, *refs):
    parts, hidden = refs[:-1], refs[-1]
    width = w_gate.shape[1]
    step = max(n for n in range(LANES, 1025, LANES) if width % n == 0)
    gate = up = None
    for c in range(0, width, step):
        rows = stacked(parts, slice(c, c + step))
        g = jnp.dot(rows, w_gate[0, c : c + step, :], preferred_element_type=F32)
        u = jnp.dot(rows, w_up[0, c : c + step, :], preferred_element_type=F32)
        gate = g if gate is None else gate + g
        up = u if up is None else up + u
    hidden[...] = (gate / (1.0 + jnp.exp(-gate)) * up).astype(BF16)


def down_kernel(expert, w_down, hidden, *refs):
    parts, outs = refs[:-4], refs[-4:]
    low = outs[0].shape[0]
    coef = stacked(parts, slice(-LANES, None)).astype(F32)
    lane = lax.broadcasted_iota(jnp.int32, coef.shape, 1)
    coef = jnp.sum(jnp.where(lane == expert[0], coef, 0.0), axis=1, keepdims=True)
    width = w_down.shape[2]
    step = max(n for n in range(LANES, 1025, LANES) if width % n == 0)
    h = hidden[...]
    for c in range(0, width, step):
        part = coef * jnp.dot(
            h, w_down[0, :, c : c + step], preferred_element_type=F32
        )
        for i, out in enumerate(outs):
            out[:, c : c + step] = part[i * low : (i + 1) * low].astype(out.dtype)


def shards(tokens, expert_ids, route_weights, w_gate, w_up, w_down):
    tok_rows, width = tokens.shape
    hid = w_gate.shape[2]
    node_count = lax.axis_size("node")
    local_count = lax.axis_size("local")
    split_count = node_count * local_count // EXPERTS
    bits = local_count.bit_length() - 1
    dims = level_bits(node_count, bits)[::-1]
    half = tok_rows * local_count
    rows = 2 * half
    me = lax.axis_index("node") * local_count + lax.axis_index("local")
    expert = (me // split_count).astype(jnp.int32).reshape(1)

    side = local_count // 2
    masks = [
        sum(1 << k for k in range(bits - 1) if i >> (bits - 2 - k) & 1)
        for i in range(side)
    ]
    block = prepare(expert, tokens, expert_ids, route_weights, w_down)
    far = [swap(block, dims[-1], local_count)]
    near = [block] + [swap_across(block, dims, m, local_count) for m in range(1, side)]
    far += [swap_across(far[0], dims, m, local_count) for m in masks[1:]]
    near = join(near, (w_down,), ())
    far = join(far, (w_down,))
    mine = [near, far]
    parts = mine + [swap_core(m, node_count) for m in mine]

    w_gate, w_up, w_down = in_vmem(w_gate), in_vmem(w_up), in_vmem(w_down)
    hidden = call(
        proj_kernel,
        [VM((rows, hid), BF16)],
        w_gate,
        w_up,
        *parts,
        limit=4,
        flops=4 * rows * hid * width,
        nbytes=4 * hid * width,
    )[0]
    low = half // 2
    own_low, own_high, other_low, other_high = call(
        down_kernel,
        [VM((low, width), kind) for kind in (F32, F32, BF16, BF16)],
        w_down,
        hidden,
        *parts,
        scalars=(expert,),
        limit=4,
        flops=2 * rows * hid * width,
        nbytes=2 * hid * width,
    )
    def halve(total, dim):
        n = total.shape[0] // 2
        return total[:n] + swap(total[n:].astype(BF16), dim, local_count).astype(F32)

    def gather_side(rows):
        total = rows[:tok_rows]
        for i in [*range(2, local_count // 2 - 1), 1, local_count // 2 - 1]:
            part = rows[i * tok_rows : (i + 1) * tok_rows].astype(BF16)
            mask = sum(1 << k for k in range(bits - 1) if i >> (bits - 2 - k) & 1)
            total = total + swap_across(part, dims, mask, local_count).astype(F32)
        return total

    far = own_high + swap_core(other_high, node_count).astype(F32)
    near = own_low + swap_core(other_low, node_count).astype(F32)
    far = gather_side(far)
    for dim in dims[-2::-1]:
        near = halve(near, dim)
    far = swap(far.astype(BF16), dims[-1], local_count)
    return (near + far.astype(F32)).astype(BF16)


def solution(mesh):
    return jax.shard_map(
        shards,
        mesh=mesh,
        in_specs=(
            P(("groups", "node", "local"), None),
            P(("groups", "node", "local"), None),
            P(("groups", "node", "local"), None),
            P(("node", "local"), None, None),
            P(("node", "local"), None, None),
            P(("node", "local"), None, None),
        ),
        out_specs=P(("groups", "node", "local"), None),
        check_vma=False,
    )
```
